1024 devices in a mesh: lat: 64 (over z, y), lon: 16 (over x, core).
Axes of the slice: x: 8, y: 8, z: 8, core: 2. Of those that a mesh axis runs over, the one named last changes fastest.
Arguments:
- saved_input: bfloat16 [640, 384, 2048], P('lat', None, 'lon'), may hold values from -0.1875 to 0.1875
- saved_spectra: bfloat16 [384, 384, 2048], P('lat', None, 'lon'), may hold values from -6 to 6
- out_grad: bfloat16 [384, 384, 2048], P('lat', None, 'lon'), may hold values from -0.1875 to 0.1875
- legendre: bfloat16 [384, 384, 640], P('lat'), may hold values from -0.3125 to 0.3125
- spectral_gain: float32 [384, 256], P(None, 'lon'), may hold values from 0.25 to 4
- band_filter: bfloat16 [640, 13], replicated, may hold values from -24 to 24
- band_start: int32 [640], replicated, may hold values from 0 to 638, as said below
- band_width: int32 [640], replicated, may hold values from 2 to 13, as said below
- slot_order: int32 [384], replicated, may hold values from 0 to 383, each once
Outputs:
- input_grad: bfloat16 [640, 384, 2048], P('lat', None, 'lon')
- gain_grad: float32 [384, 256], P(None, 'lon')
- filter_grad: float32 [640, 13], P('lat')
The draws below stay inside these ranges and needn't reach their ends.
Inputs may be any that keep to these rules, and one draw needn't show every extreme that they name: Row i's support, rows band_start[i] to band_start[i] + band_width[i] - 1, contains i and lies in the grid and within 6 rows of i; every row but the first reaches at least one row below itself. `band_width`: some row's support has exactly 13 rows. `slot_order`: each order stands in exactly one slot.
All inputs are finite; a program needn't handle non-finite values.
Results may differ from the reference program's by a relative error of at most 0.0057.
Values may be sent and summed in bfloat16 or wider, within the bound.
A program may use at most 64 MiB of HBM per device.

```python
import math
import jax
import jax.numpy as jnp
from jax import lax

C = 256
M = 384
L = 384
BATCH = 4
REACH = 6
NLAT = 640
WMAX = 13
LANES = 2048
N_LON = 16


def band_rows(key):
    base_key = jax.random.fold_in(key, 31)
    key_below, key_above, key_widest = jax.random.split(base_key, 3)
    row_index = jnp.arange(NLAT, dtype=jnp.int32)
    cap_rows = max(NLAT // 8, 1)
    polar = (row_index < cap_rows) | (row_index >= NLAT - cap_rows)
    reach_below = jax.random.randint(key_below, (NLAT,), 1, REACH + 1)
    reach_above = jax.random.randint(key_above, (NLAT,), 1, REACH + 1)
    reach_below = jnp.where(polar, reach_below, (reach_below + 1) // 2)
    reach_above = jnp.where(polar, reach_above, (reach_above + 1) // 2)
    widest = jax.random.randint(key_widest, (), REACH, NLAT - REACH)
    reach_below = jnp.where(row_index == widest, REACH, reach_below)
    reach_above = jnp.where(row_index == widest, REACH, reach_above)
    reach_below = jnp.where(row_index == NLAT - 1, 1, reach_below)
    first_row = jnp.maximum(row_index - reach_below, 0)
    last_row = jnp.minimum(row_index + reach_above, NLAT - 1)
    return (first_row.astype(jnp.int32), (last_row - first_row + 1).astype(jnp.int32))


def draw_band_start(key, part):
    return band_rows(key)[0]


def draw_band_width(key, part):
    return band_rows(key)[1]


def steps_of(own_key, dims, cuts, smallest, top_value):
    def one(dim, parts):
        steps = jax.random.uniform(jax.random.fold_in(jax.random.fold_in(own_key, 6), dim), (parts,), jnp.float32, smallest / len(cuts), top_value / len(cuts))
        return jnp.repeat(jnp.exp(steps), dims[dim] // parts).reshape((-1,) + (1,) * (len(dims) - dim - 1))

    loudness = one(*cuts[0])
    for cut in cuts[1:]:
        loudness = loudness * one(*cut)
    return loudness


def centred(stream_key, shape, deviation, limit, cuts=(), kind=jnp.bfloat16):
    loudness = steps_of(stream_key, shape, cuts, -0.22, 0.18) if cuts else 1.0
    entries = jax.random.normal(stream_key, shape, jnp.float32) * deviation * loudness
    return jnp.minimum(jnp.maximum(entries, -limit), limit).astype(kind)


def setup_inputs(seed: int = 0) -> dict:
    key_of = jax.random.split(jax.random.key(seed), 10)
    return {
        "saved_input": centred(key_of[0], (NLAT, M, LANES), 0.03, 0.1875, ((0, 64), (2, 16))),
        "saved_spectra": centred(key_of[1], (M, L, LANES), 1.0, 6.0, ((0, 64), (2, 16))),
        "out_grad": centred(key_of[2], (M, L, LANES), 0.03, 0.1875, ((0, 64), (2, 16))),
        "legendre": centred(key_of[3], (M, L, NLAT), L ** -0.5, 0.3125, ((0, 64),)),
        "spectral_gain": jnp.clip(jnp.exp(math.log(4.0) - 2.7725887 * jax.random.uniform(key_of[4], (L, C), jnp.float32) ** steps_of(key_of[4], (L, C), ((1, 16),), -0.2, 0.2)), 0.25, 4.0),
        "band_filter": centred(key_of[5], (NLAT, WMAX), 4.0, 24.0),
        "band_start": draw_band_start(jax.random.fold_in(key_of[9], 71), 0),
        "band_width": draw_band_width(jax.random.fold_in(key_of[9], 71), 0),
        "slot_order": jax.random.permutation(key_of[8], M).astype(jnp.int32),
    }


def reference(saved_input, saved_spectra, out_grad, legendre, spectral_gain, band_filter, band_start, band_width, slot_order):
    per_channel = 2 * BATCH
    block_count = N_LON
    block_width = C // block_count
    block_lanes = block_width * per_channel
    degrees = jnp.arange(L, dtype=jnp.int32)
    keep_mask = (degrees[None, :] >= slot_order[:, None]).astype(jnp.float32)
    slot_of = jnp.zeros((M,), jnp.int32).at[slot_order].set(jnp.arange(M, dtype=jnp.int32))
    legendre_wide = legendre.astype(jnp.float32)
    row_index = jnp.arange(NLAT, dtype=jnp.int32)
    source_rows = row_index[:, None] + jnp.arange(WMAX, dtype=jnp.int32)[None, :] - REACH
    inside = (source_rows >= 0) & (source_rows < NLAT)
    clipped = jnp.clip(source_rows, 0, NLAT - 1)
    tap_index = row_index[:, None] - band_start[clipped]
    is_valid = inside & (tap_index >= 0) & (tap_index < band_width[clipped])
    tap_weights = jnp.where(is_valid, band_filter[clipped, jnp.clip(tap_index, 0, WMAX - 1)].astype(jnp.float32), 0.0)

    def one_block(filter_total, block_id):
        lane_first = block_id * block_lanes
        grad_block = lax.dynamic_slice_in_dim(out_grad, lane_first, block_lanes, 2).astype(jnp.float32) * keep_mask[:, :, None]
        spectra_block = lax.dynamic_slice_in_dim(saved_spectra, lane_first, block_lanes, 2).astype(jnp.float32)
        gain_block = lax.dynamic_slice_in_dim(spectral_gain, block_id * block_width, block_width, 1)
        gain_part = jnp.sum((grad_block * spectra_block).reshape(M, L, block_width, per_channel), axis=(0, 3))
        spec_grad = (grad_block * jnp.repeat(gain_block, per_channel, axis=1)[None]).astype(jnp.bfloat16)
        slot_grad = jnp.einsum("kli,kln->kin", legendre_wide, spec_grad.astype(jnp.float32)).astype(jnp.bfloat16)
        lat_grad = jnp.transpose(jnp.take(slot_grad, slot_of, axis=0), (1, 0, 2))
        grad_wide = lat_grad.astype(jnp.float32)
        padded = jnp.pad(grad_wide, ((REACH, REACH), (0, 0), (0, 0)))
        input_part = jnp.zeros((NLAT, M, block_lanes), jnp.float32)
        for offset in range(WMAX):
            input_part = input_part + tap_weights[:, offset][:, None, None] * padded[offset:offset + NLAT]
        input_block = lax.dynamic_slice_in_dim(saved_input, lane_first, block_lanes, 2).astype(jnp.float32)
        columns = []
        for offset in range(WMAX):
            source = jnp.clip(band_start + offset, 0, NLAT - 1)
            columns.append(jnp.sum(grad_wide * jnp.take(input_block, source, axis=0), axis=(1, 2)))
        taps_live = jnp.arange(WMAX, dtype=jnp.int32)[None, :] < band_width[:, None]
        filter_part = jnp.where(taps_live, jnp.stack(columns, axis=1), 0.0)
        return filter_total + filter_part, (gain_part, input_part.astype(jnp.bfloat16))

    filter_grad, (gain_parts, input_parts) = lax.scan(one_block, jnp.zeros((NLAT, WMAX), jnp.float32), jnp.arange(block_count, dtype=jnp.int32))
    gain_grad = jnp.transpose(gain_parts, (1, 0, 2)).reshape(L, C)
    input_grad = jnp.transpose(input_parts, (1, 2, 0, 3)).reshape(NLAT, M, 2 * BATCH * C)
    return input_grad, gain_grad, filter_grad
```

```python
import functools
import jax
import jax.numpy as jnp
from jax import lax
from jax.sharding import PartitionSpec as P
from jax.experimental import pallas as pl
from jax.experimental.pallas import tpu as pltpu

MESH = pl.DeviceIdType.MESH
HIGHEST = lax.Precision.HIGHEST
F32 = jnp.float32
BF16 = jnp.bfloat16
I32 = jnp.int32

RING = 8
SLOTS = 2
CHUNKS = 3
ORIENT = ("y", "z", "z")
TILE = RING * SLOTS
REACH = 6
ROWS = 10
PLANE = RING * ROWS
WINDOW = 24
FAR_FIRST = (4, 3, 5, 2, 6, 1, 7)


def iota(shape, dim):
    return lax.broadcasted_iota(I32, shape, dim)


def dot(a, b, contract=((1,), (0,)), precision=None):
    return lax.dot_general(
        a, b, (contract, ((), ())), preferred_element_type=F32, precision=precision
    )


def kernel(
    lon_count,
    sv_hbm,
    sp_hbm,
    og_hbm,
    leg_hbm,
    gain_ref,
    filt_ref,
    start_ref,
    width_ref,
    order_ref,
    order_row_ref,
    ig_hbm,
    gg_ref,
    fg_ref,
    sv,
    sp,
    og,
    leg,
    sent,
    got,
    turned,
    window,
    sv_slots,
    ig_slots,
    pick,
    out_rows,
    gain_mine,
    gain_got,
    gain_part,
    gain_got2,
    gain_all,
    filt_mine,
    filt_got,
    filt_sum,
    filt_all,
    load_sems,
    own_sems,
    out_sems,
    p1_send,
    p1_recv,
    p2_send,
    p2_recv,
    halo_send,
    halo_recv,
    g1_send,
    g1_recv,
    g2_send,
    g2_recv,
    g3_send,
    g3_recv,
    f1_send,
    f1_recv,
    f2_send,
    f2_recv,
):
    p = lax.axis_index("lat")
    q = lax.axis_index("lon")
    z, y = p // RING, lax.rem(p, RING)
    lat_count = RING * RING

    def z_peer(d):
        return lax.rem(z + d, RING) * RING + y

    def y_peer(d):
        return z * RING + lax.rem(y + d, RING)

    peer_of = {"z": z_peer, "y": y_peer}
    place_of = {"z": z, "y": y}
    other = {"z": "y", "y": "z"}
    up = lax.rem(p + 1, lat_count)
    down = lax.rem(p + lat_count - 1, lat_count)

    def remote(src, dst, s, r, lat):
        return pltpu.make_async_remote_copy(
            src_ref=src,
            dst_ref=dst,
            send_sem=s,
            recv_sem=r,
            device_id={"lat": lat},
            device_id_type=MESH,
        )

    loads = {}

    def load(name, index, src, dst):
        cp = pltpu.make_async_copy(src, dst, load_sems.at[index])
        cp.start()
        loads[name] = cp

    for c in range(CHUNKS):
        part = pl.ds(SLOTS * c, SLOTS)
        load(("og", c), 2 * c, og_hbm.at[part], og.at[part])
        load(("leg", c), 2 * c + 1, leg_hbm.at[part], leg.at[part])
    load("sp", 6, sp_hbm, sp)
    load("sv", 7, sv_hbm, sv)

    barrier = pltpu.get_barrier_semaphore()
    for d in range(1, RING):
        for axis in ("z", "y"):
            pl.semaphore_signal(
                barrier, inc=1, device_id={"lat": peer_of[axis](d)}, device_id_type=MESH
            )
    for lat in (up, down):
        pl.semaphore_signal(barrier, inc=1, device_id={"lat": lat}, device_id_type=MESH)
    for d in range(1, lon_count):
        pl.semaphore_signal(
            barrier,
            inc=1,
            device_id={"lon": lax.rem(q + d, lon_count)},
            device_id_type=MESH,
        )

    degrees = sp.shape[1]
    lanes = sp.shape[2]
    channels = gain_ref.shape[1]
    per_channel = lanes // channels
    lat_rows = lat_count * ROWS

    spread = (iota((channels, lanes), 1) // per_channel == iota((channels, lanes), 0)).astype(F32)
    lane_gain = dot(gain_ref[...], spread, precision=HIGHEST)

    degree = iota((degrees, lanes), 0)

    def turn_rows():
        row = iota((lat_rows, 128), 0)
        tens = lax.shift_right_logical(row * 6554, 16)
        rest = row - tens * ROWS
        major = lax.shift_right_logical(tens, 3)
        minor = tens & 7
        target = minor * PLANE + major * ROWS + rest
        lane = iota((lat_rows, 128), 1)
        return jnp.concatenate(
            [(target == lane + 128 * b).astype(BF16) for b in range(lat_rows // 128)], axis=1
        )

    rows_turned = turn_rows() if "y" in ORIENT else None

    def make_chunk(c):
        loads["og", c].wait()
        loads["leg", c].wait()
        for s in range(SLOTS):
            k = SLOTS * c + s
            keep = degree >= order_ref[p * (SLOTS * CHUNKS) + k]
            masked = jnp.where(keep, og[k].astype(F32), 0.0)
            spec = (masked * lane_gain).astype(BF16)
            grad = dot(leg[k], spec, ((0,), (0,))).astype(BF16)
            if ORIENT[c] == "y":
                grad = dot(rows_turned, grad).astype(BF16)
            for t in range(RING):
                sent[c, t, s] = grad[t * PLANE : (t + 1) * PLANE]

    phase1 = {}
    phase2 = {}
    halo = {}

    def send_phase1(c):
        axis = ORIENT[c]
        me = place_of[axis]
        cps = []
        for n, d in enumerate(FAR_FIRST):
            target = lax.rem(me + d, RING)
            cp = remote(
                sent.at[c, target], got.at[c, me], p1_send.at[c, n], p1_recv.at[c, n], peer_of[axis](d)
            )
            cp.start()
            cps.append(cp)
        got[c, me] = sent[c, me]
        phase1[c] = cps

    a, b = iota((256, 256), 0), iota((256, 256), 1)
    swap = ((a & 15) * 16 + lax.shift_right_logical(a, 4) == b).astype(BF16)

    def turn(c):
        for cp in phase1[c]:
            cp.wait_recv()
        for blk in range(PLANE // 16):
            x = got[c, :, :, blk * 16 : (blk + 1) * 16, :].reshape(256, lanes)
            turned[c, blk * 16 : (blk + 1) * 16] = dot(swap, x).astype(BF16).reshape(16, TILE, lanes)

    def send_phase2(c):
        axis = other[ORIENT[c]]
        me = place_of[axis]
        cps = []
        for n, d in enumerate(FAR_FIRST):
            target = lax.rem(me + d, RING)
            cp = remote(
                turned.at[c, pl.ds(target * ROWS, ROWS)],
                window.at[c, me, pl.ds(REACH, ROWS)],
                p2_send.at[c, n],
                p2_recv.at[c, n],
                peer_of[axis](d),
            )
            cp.start()
            cps.append(cp)
        window[c, me, REACH : REACH + ROWS] = turned[c, pl.ds(me * ROWS, ROWS)]
        phase2[c] = cps

    def send_halo(c):
        for cp in phase2[c]:
            cp.wait_recv()
        cps = [
            remote(
                window.at[c, :, pl.ds(ROWS, REACH)],
                window.at[c, :, pl.ds(0, REACH)],
                halo_send.at[c, 0],
                halo_recv.at[c, 0],
                up,
            ),
            remote(
                window.at[c, :, pl.ds(REACH, REACH)],
                window.at[c, :, pl.ds(REACH + ROWS, REACH)],
                halo_send.at[c, 1],
                halo_recv.at[c, 1],
                down,
            ),
        ]
        for cp in cps:
            cp.start()
        halo[c] = cps

    make_chunk(0)
    pl.semaphore_wait(barrier, 2 * (RING - 1) + 2 + lon_count - 1)
    send_phase1(0)
    make_chunk(1)
    send_phase1(1)
    make_chunk(2)

    loads["sp"].wait()
    total = jnp.zeros((degrees, lanes), F32)
    for k in range(SLOTS * CHUNKS):
        keep = degree >= order_ref[p * (SLOTS * CHUNKS) + k]
        masked = jnp.where(keep, og[k].astype(F32), 0.0)
        total = total + masked * sp[k].astype(F32)
    groups = degrees // 64
    packed = jnp.zeros((64, 128), F32)
    lane_from, lane_to = iota((lanes, 128), 0), iota((lanes, 128), 1)
    for g in range(groups):
        fold = (lane_from // per_channel + channels * g == lane_to).astype(F32)
        packed = packed + dot(total[64 * g : 64 * (g + 1)], fold, precision=HIGHEST)
    gain_mine[...] = packed.reshape(RING, 8, 128)
    gain1 = []
    for n, d in enumerate(FAR_FIRST):
        cp = remote(
            gain_mine.at[lax.rem(z + d, RING)], gain_got.at[z], g1_send.at[n], g1_recv.at[n], z_peer(d)
        )
        cp.start()
        gain1.append(cp)
    gain_got[z] = gain_mine[z]

    k = iota((degrees, degrees), 0)
    lat_of = lax.shift_right_logical(k * 10923, 16)
    rest = k - lat_of * (SLOTS * CHUNKS)
    chunk_of, s_of = lax.shift_right_logical(rest, 1), rest & 1
    z_of, y_of = lax.shift_right_logical(lat_of, 3), lat_of & 7
    z_first = y_of * TILE + z_of * SLOTS + s_of
    y_first = z_of * TILE + y_of * SLOTS + s_of
    column = z_first
    for c in range(CHUNKS):
        if ORIENT[c] == "y":
            column = jnp.where(chunk_of == c, y_first, column)
    column = column + chunk_of * 128
    arrive = (column == iota((degrees, degrees), 1)).astype(F32)
    order_row = jnp.broadcast_to(order_row_ref[...].astype(F32), (8, degrees))
    order_arrive = dot(order_row, arrive, precision=HIGHEST)[0:1]
    pick_f32 = (
        iota((degrees, degrees), 0).astype(F32) == jnp.broadcast_to(order_arrive, (degrees, degrees))
    ).astype(F32)
    pick[...] = pick_f32.astype(BF16)
    pick_t = pick_f32.T.astype(BF16)

    turn(1)
    send_phase2(1)
    send_phase1(2)

    loads["sv"].wait()
    for j in range(0, ROWS, 2):
        pair = jnp.concatenate([sv[j], sv[j + 1]], axis=1)
        moved = dot(pick_t, pair).astype(BF16)
        sv_slots[j] = moved[:, :lanes]
        sv_slots[j + 1] = moved[:, lanes:]

    turn(0)

    first = p * ROWS
    e_row = iota((WINDOW, 128), 0)
    lane = iota((WINDOW, 128), 1)
    starts = jnp.zeros((WINDOW, 128), I32)
    widths = jnp.zeros((WINDOW, 128), I32)
    for e in range(ROWS + 2 * REACH):
        row = jnp.clip(first - REACH + e, 0, lat_rows - 1)
        starts = jnp.where(e_row == e, start_ref[row], starts)
        widths = jnp.where(e_row == e, width_ref[row], widths)
    row_e = e_row + (first - REACH)
    inside = (row_e >= 0) & (row_e < lat_rows) & (e_row < ROWS + 2 * REACH)
    widths = jnp.where(inside, widths, 0)
    row_pick = (iota((WINDOW, lat_rows), 1) == iota((WINDOW, lat_rows), 0) + (first - REACH)).astype(BF16)
    taps = dot(row_pick, filt_ref[...])
    tap_count = taps.shape[1]
    tap = lane + first - starts
    band = jnp.zeros((WINDOW, 128), F32)
    for t in range(tap_count):
        hit = (tap == t) & (t < widths)
        band = jnp.where(hit, jnp.broadcast_to(taps[:, t : t + 1], (WINDOW, 128)), band)
    pick_j = (lax.shift_right_logical(iota((ROWS * TILE, 128), 0), 4) == iota((ROWS * TILE, 128), 1)).astype(BF16)
    pick_e = (lax.shift_right_logical(iota((WINDOW, WINDOW * TILE), 1), 4) == iota((WINDOW, WINDOW * TILE), 0)).astype(BF16)
    wide = dot(pick_j, band.astype(BF16), ((1,), (1,))).astype(BF16)
    wide = dot(wide, pick_e)
    same_slot = (iota((ROWS * TILE, WINDOW * TILE), 0) & 15) == (iota((ROWS * TILE, WINDOW * TILE), 1) & 15)
    band_wide = jnp.where(same_slot, wide, 0.0).astype(BF16)

    for c in range(CHUNKS):
        window[c, :, ROWS + 2 * REACH : WINDOW] = jnp.zeros(
            (RING, WINDOW - ROWS - 2 * REACH, TILE, lanes), BF16
        )

    turn(2)
    send_phase2(2)
    send_phase2(0)

    for cp in gain1:
        cp.wait_recv()
    gain_part[...] = jnp.sum(gain_got[...], axis=0)
    gain2 = []
    for n, d in enumerate(FAR_FIRST):
        cp = remote(gain_part, gain_got2.at[y], g2_send.at[n], g2_recv.at[n], y_peer(d))
        cp.start()
        gain2.append(cp)
    gain_got2[y] = gain_part[...]

    gram = jnp.zeros((WINDOW * TILE, ROWS * TILE), F32)

    def finish_chunk(c, gram):
        for cp in halo[c]:
            cp.wait_recv()
        tiles, sides = [], []
        for t in range(RING):
            x = window[c, t].reshape(WINDOW * TILE, lanes)
            lo = c * 128 + t * TILE
            ig_slots[:, lo : lo + TILE, :] = dot(band_wide, x).astype(BF16).reshape(ROWS, TILE, lanes)
            tiles.append(x)
            sides.append(sv_slots[:, lo : lo + TILE, :].reshape(ROWS * TILE, lanes))
        return gram + dot(jnp.concatenate(tiles, axis=1), jnp.concatenate(sides, axis=1), ((1,), (1,)))

    send_halo(1)
    gram = finish_chunk(1, gram)
    send_halo(0)
    for cp in gain2:
        cp.wait_recv()
    gain_mine_sum = jnp.sum(gain_got2[...], axis=0)
    gain_all[z] = gain_mine_sum
    gain3 = []
    for n, d in enumerate(FAR_FIRST):
        cp = remote(gain_all.at[z], gain_all.at[z], g3_send.at[n], g3_recv.at[n], z_peer(d))
        cp.start()
        gain3.append(cp)
    send_halo(2)
    gram = finish_chunk(0, gram)
    for cp in gain3:
        cp.wait_recv()
    summed = gain_all[...].reshape(64, 128)
    for g in range(groups):
        gg_ref[64 * g : 64 * (g + 1), :] = summed[:, channels * g : channels * (g + 1)]
    gram = finish_chunk(2, gram)

    diagonal = (iota(gram.shape, 0) & 15) == (iota(gram.shape, 1) & 15)
    gram = jnp.where(diagonal, gram, 0.0)
    by_j = (lax.shift_right_logical(iota((ROWS * TILE, 128), 0), 4) == iota((ROWS * TILE, 128), 1)).astype(F32)
    by_e = (lax.shift_right_logical(iota((WINDOW, WINDOW * TILE), 1), 4) == iota((WINDOW, WINDOW * TILE), 0)).astype(F32)
    small = dot(dot(by_e, gram, precision=HIGHEST), by_j, precision=HIGHEST)
    part = jnp.zeros((WINDOW, 128), F32)
    for j in range(ROWS):
        hit = (lane + starts == first + j) & (lane < widths)
        part = part + jnp.where(hit, jnp.broadcast_to(small[:, j : j + 1], (WINDOW, 128)), 0.0)
    filt_mine[...] = part
    filt1 = [
        remote(filt_mine, filt_got.at[0], f1_send.at[0], f1_recv.at[0], up),
        remote(filt_mine, filt_got.at[1], f1_send.at[1], f1_recv.at[1], down),
    ]
    for cp in filt1:
        cp.start()

    writes = []
    for j in range(0, ROWS, 2):
        if j == 4:
            for cp in filt1:
                cp.wait_recv()
            filt_sum[...] = jnp.zeros(filt_sum.shape, F32)
            filt_sum[0:ROWS] = filt_mine[REACH : REACH + ROWS]
            filt_sum[0:REACH] += filt_got[0, REACH + ROWS : ROWS + 2 * REACH]
            filt_sum[ROWS - REACH : ROWS] += filt_got[1, 0:REACH]
            filt_all[q] = filt_sum[...]
            filt2 = []
            for d in range(1, lon_count):
                cp = pltpu.make_async_remote_copy(
                    src_ref=filt_all.at[q],
                    dst_ref=filt_all.at[q],
                    send_sem=f2_send.at[d - 1],
                    recv_sem=f2_recv.at[d - 1],
                    device_id={"lon": lax.rem(q + d, lon_count)},
                    device_id_type=MESH,
                )
                cp.start()
                filt2.append(cp)
        pair = jnp.concatenate([ig_slots[j], ig_slots[j + 1]], axis=1)
        moved = dot(pick[...], pair).astype(BF16)
        out_rows[j] = moved[:, :lanes]
        out_rows[j + 1] = moved[:, lanes:]
        cp = pltpu.make_async_copy(
            out_rows.at[pl.ds(j, 2)], ig_hbm.at[pl.ds(j, 2)], out_sems.at[j // 2]
        )
        cp.start()
        writes.append(cp)

    for cp in filt2:
        cp.wait_recv()
    fg_ref[...] = jnp.sum(filt_all[...], axis=0)[:ROWS, :tap_count]
    for cps in [*phase1.values(), *phase2.values(), *halo.values(), gain1, gain2, gain3, filt1, filt2]:
        for cp in cps:
            cp.wait_send()
    for cp in writes:
        cp.wait()


def per_device(sv, sp, og, leg, gain, filt, start, width, order):
    lon_count = lax.axis_size("lon")
    slots, degrees, lanes = sp.shape
    rows, orders = sv.shape[0], sv.shape[1]
    lat_rows, tap_count = filt.shape
    any_space = pl.BlockSpec(memory_space=pl.ANY)
    vmem = pl.BlockSpec(memory_space=pltpu.VMEM)
    smem = pl.BlockSpec(memory_space=pltpu.SMEM)
    dma = pltpu.SemaphoreType.DMA
    peers = RING - 1
    return pl.pallas_call(
        functools.partial(kernel, lon_count),
        out_shape=(
            jax.ShapeDtypeStruct(sv.shape, BF16),
            jax.ShapeDtypeStruct(gain.shape, F32),
            jax.ShapeDtypeStruct((rows, tap_count), F32),
        ),
        in_specs=[any_space] * 4 + [vmem] * 2 + [smem] * 3 + [vmem],
        out_specs=(any_space, vmem, vmem),
        scratch_shapes=[
            pltpu.VMEM(sv.shape, BF16),
            pltpu.VMEM(sp.shape, BF16),
            pltpu.VMEM(og.shape, BF16),
            pltpu.VMEM(leg.shape, BF16),
            pltpu.VMEM((CHUNKS, RING, SLOTS, PLANE, lanes), BF16),
            pltpu.VMEM((CHUNKS, RING, SLOTS, PLANE, lanes), BF16),
            pltpu.VMEM((CHUNKS, PLANE, TILE, lanes), BF16),
            pltpu.VMEM((CHUNKS, RING, WINDOW, TILE, lanes), BF16),
            pltpu.VMEM((rows, orders, lanes), BF16),
            pltpu.VMEM((rows, orders, lanes), BF16),
            pltpu.VMEM((orders, orders), BF16),
            pltpu.VMEM((rows, orders, lanes), BF16),
            pltpu.VMEM((RING, 8, 128), F32),
            pltpu.VMEM((RING, 8, 128), F32),
            pltpu.VMEM((8, 128), F32),
            pltpu.VMEM((RING, 8, 128), F32),
            pltpu.VMEM((RING, 8, 128), F32),
            pltpu.VMEM((WINDOW, 128), F32),
            pltpu.VMEM((2, WINDOW, 128), F32),
            pltpu.VMEM((16, 128), F32),
            pltpu.VMEM((lon_count, 16, 128), F32),
            dma((8,)),
            dma((1,)),
            dma((rows // 2,)),
            dma((CHUNKS, peers)),
            dma((CHUNKS, peers)),
            dma((CHUNKS, peers)),
            dma((CHUNKS, peers)),
            dma((CHUNKS, 2)),
            dma((CHUNKS, 2)),
            dma((peers,)),
            dma((peers,)),
            dma((peers,)),
            dma((peers,)),
            dma((peers,)),
            dma((peers,)),
            dma((2,)),
            dma((2,)),
            dma((lon_count - 1,)),
            dma((lon_count - 1,)),
        ],
        compiler_params=pltpu.CompilerParams(
            collective_id=0, has_side_effects=True, vmem_limit_bytes=48 * 2**20
        ),
        name="backward",
    )(sv, sp, og, leg, gain, filt, start, width, order, order.reshape(1, -1))


def solution(mesh):
    return jax.shard_map(
        per_device,
        mesh=mesh,
        in_specs=(
            P("lat", None, "lon"),
            P("lat", None, "lon"),
            P("lat", None, "lon"),
            P("lat", None, None),
            P(None, "lon"),
            P(),
            P(),
            P(),
            P(),
        ),
        out_specs=(P("lat", None, "lon"), P(None, "lon"), P("lat", None)),
        check_vma=False,
    )
```

```python
import functools
import jax
import jax.numpy as jnp
from jax import lax
from jax.sharding import PartitionSpec as P
from jax.experimental import pallas as pl
from jax.experimental.pallas import tpu as pltpu

MESH = pl.DeviceIdType.MESH
HIGHEST = lax.Precision.HIGHEST
F32 = jnp.float32
BF16 = jnp.bfloat16
I32 = jnp.int32

RING = 8
SLOTS = 2
CHUNKS = 3
ORIENT = ("y", "z", "y")
TILE = RING * SLOTS
REACH = 6
ROWS = 10
PLANE = RING * ROWS
WINDOW = 24
FAR_FIRST = (4, 3, 5, 2, 6, 1, 7)


def iota(shape, dim):
    return lax.broadcasted_iota(I32, shape, dim)


def dot(a, b, contract=((1,), (0,)), precision=None):
    return lax.dot_general(
        a, b, (contract, ((), ())), preferred_element_type=F32, precision=precision
    )


def kernel(
    lon_count,
    sv_hbm,
    sp_hbm,
    og_hbm,
    leg_hbm,
    gain_ref,
    filt_ref,
    start_hbm,
    width_hbm,
    order_hbm,
    ig_hbm,
    gg_ref,
    fg_ref,
    sv,
    sp,
    og,
    leg,
    sent,
    got,
    turned,
    window,
    sv_slots,
    ig_slots,
    pick,
    placed,
    out_rows,
    start_ref,
    width_ref,
    order_ref,
    order_row_ref,
    gain_mine,
    gain_got,
    gain_part,
    gain_got2,
    gain_all,
    filt_mine,
    filt_got,
    filt_sum,
    filt_all,
    load_sems,
    out_sems,
    p1_send,
    p1_recv,
    p2_send,
    p2_recv,
    halo_send,
    halo_recv,
    g1_send,
    g1_recv,
    g2_send,
    g2_recv,
    g3_send,
    g3_recv,
    f1_send,
    f1_recv,
    f2_send,
    f2_recv,
):
    p = lax.axis_index("lat")
    q = lax.axis_index("lon")
    z, y = p // RING, lax.rem(p, RING)
    lat_count = RING * RING

    def z_peer(d):
        return lax.rem(z + d, RING) * RING + y

    def y_peer(d):
        return z * RING + lax.rem(y + d, RING)

    peer_of = {"z": z_peer, "y": y_peer}
    place_of = {"z": z, "y": y}
    other = {"z": "y", "y": "z"}
    up = lax.rem(p + 1, lat_count)
    down = lax.rem(p + lat_count - 1, lat_count)

    def remote(src, dst, s, r, lat):
        return pltpu.make_async_remote_copy(
            src_ref=src,
            dst_ref=dst,
            send_sem=s,
            recv_sem=r,
            device_id={"lat": lat},
            device_id_type=MESH,
        )

    loads = {}

    def load(name, index, src, dst):
        cp = pltpu.make_async_copy(src, dst, load_sems.at[index])
        cp.start()
        loads[name] = cp

    load("order", 8, order_hbm, order_ref)
    for c in range(CHUNKS):
        part = pl.ds(SLOTS * c, SLOTS)
        load(("og", c), 2 * c, og_hbm.at[part], og.at[part])
        load(("leg", c), 2 * c + 1, leg_hbm.at[part], leg.at[part])
    load("sp", 6, sp_hbm, sp)
    load("sv", 7, sv_hbm, sv)
    load("row", 9, order_hbm, order_row_ref)
    load("start", 10, start_hbm, start_ref)
    load("width", 11, width_hbm, width_ref)

    barrier = pltpu.get_barrier_semaphore()
    for d in range(1, RING):
        for axis in ("z", "y"):
            pl.semaphore_signal(
                barrier, inc=1, device_id={"lat": peer_of[axis](d)}, device_id_type=MESH
            )
    for lat in (up, down):
        pl.semaphore_signal(barrier, inc=1, device_id={"lat": lat}, device_id_type=MESH)
    for d in range(1, lon_count):
        pl.semaphore_signal(
            barrier,
            inc=1,
            device_id={"lon": lax.rem(q + d, lon_count)},
            device_id_type=MESH,
        )

    degrees = sp.shape[1]
    lanes = sp.shape[2]
    channels = gain_ref.shape[0]
    per_channel = lanes // channels
    lat_rows = lat_count * ROWS

    spread = (iota((channels, lanes), 1) // per_channel == iota((channels, lanes), 0)).astype(F32)
    lane_gain = dot(gain_ref[...], spread, ((0,), (0,)), precision=HIGHEST)

    degree = iota((degrees, lanes), 0)

    def turn_rows():
        row = iota((lat_rows, 128), 0)
        tens = lax.shift_right_logical(row * 6554, 16)
        rest = row - tens * ROWS
        major = lax.shift_right_logical(tens, 3)
        minor = tens & 7
        target = minor * PLANE + major * ROWS + rest
        lane = iota((lat_rows, 128), 1)
        return jnp.concatenate(
            [(target == lane + 128 * b).astype(BF16) for b in range(lat_rows // 128)], axis=1
        )

    rows_turned = turn_rows() if "y" in ORIENT else None

    def make_chunk(c):
        loads["og", c].wait()
        loads["leg", c].wait()
        for s in range(SLOTS):
            k = SLOTS * c + s
            keep = degree >= order_ref[p * (SLOTS * CHUNKS) + k]
            masked = jnp.where(keep, og[k].astype(F32), 0.0)
            spec = (masked * lane_gain).astype(BF16)
            grad = dot(leg[k], spec, ((0,), (0,))).astype(BF16)
            if ORIENT[c] == "y":
                grad = dot(rows_turned, grad).astype(BF16)
            for t in range(RING):
                sent[c, t, s] = grad[t * PLANE : (t + 1) * PLANE]

    phase1 = {}
    phase2 = {}
    halo = {}

    def send_phase1(c):
        axis = ORIENT[c]
        me = place_of[axis]
        cps = []
        for n, d in enumerate(FAR_FIRST):
            target = lax.rem(me + d, RING)
            cp = remote(
                sent.at[c, target], got.at[c, me], p1_send.at[c, n], p1_recv.at[c, n], peer_of[axis](d)
            )
            cp.start()
            cps.append(cp)
        got[c, me] = sent[c, me]
        phase1[c] = cps

    a, b = iota((256, 256), 0), iota((256, 256), 1)
    swap = ((a & 15) * 16 + lax.shift_right_logical(a, 4) == b).astype(BF16)

    def turn(c):
        for cp in phase1[c]:
            cp.wait_recv()
        for blk in range(PLANE // 16):
            x = got[c, :, :, blk * 16 : (blk + 1) * 16, :].reshape(256, lanes)
            turned[c, blk * 16 : (blk + 1) * 16] = dot(swap, x).astype(BF16).reshape(16, TILE, lanes)

    def send_phase2(c):
        axis = other[ORIENT[c]]
        me = place_of[axis]
        cps = []
        for n, d in enumerate(FAR_FIRST):
            target = lax.rem(me + d, RING)
            cp = remote(
                turned.at[c, pl.ds(target * ROWS, ROWS)],
                window.at[c, me, pl.ds(REACH, ROWS)],
                p2_send.at[c, n],
                p2_recv.at[c, n],
                peer_of[axis](d),
            )
            cp.start()
            cps.append(cp)
        window[c, me, REACH : REACH + ROWS] = turned[c, pl.ds(me * ROWS, ROWS)]
        phase2[c] = cps

    def send_halo(c):
        for cp in phase2[c]:
            cp.wait_recv()
        cps = [
            remote(
                window.at[c, :, pl.ds(ROWS, REACH)],
                window.at[c, :, pl.ds(0, REACH)],
                halo_send.at[c, 0],
                halo_recv.at[c, 0],
                up,
            ),
            remote(
                window.at[c, :, pl.ds(REACH, REACH)],
                window.at[c, :, pl.ds(REACH + ROWS, REACH)],
                halo_send.at[c, 1],
                halo_recv.at[c, 1],
                down,
            ),
        ]
        for cp in cps:
            cp.start()
        halo[c] = cps

    loads["order"].wait()
    barrier_count = 2 * (RING - 1) + 2 + lon_count - 1
    make_chunk(0)
    pl.semaphore_wait(barrier, barrier_count)
    send_phase1(0)
    make_chunk(1)
    send_phase1(1)
    make_chunk(2)
    send_phase1(2)
    loads["sp"].wait()
    total = jnp.zeros((degrees, lanes), F32)
    for k in range(SLOTS * CHUNKS):
        keep = degree >= order_ref[p * (SLOTS * CHUNKS) + k]
        masked = jnp.where(keep, og[k].astype(F32), 0.0)
        total = total + masked * sp[k].astype(F32)
    terms = dot(spread, total, ((1,), (1,)), precision=HIGHEST)
    blocks = degrees // 128
    gain_mine[...] = jnp.zeros(gain_mine.shape, F32)
    for h in range(channels // 8):
        for b in range(blocks):
            gain_mine[h * blocks + b] = terms[8 * h : 8 * h + 8, 128 * b : 128 * b + 128]
    gain1 = []
    for n, d in enumerate(FAR_FIRST):
        cp = remote(
            gain_mine.at[lax.rem(z + d, RING)], gain_got.at[z], g1_send.at[n], g1_recv.at[n], z_peer(d)
        )
        cp.start()
        gain1.append(cp)
    gain_got[z] = gain_mine[z]

    k = iota((degrees, degrees), 0)
    lat_of = lax.shift_right_logical(k * 10923, 16)
    rest = k - lat_of * (SLOTS * CHUNKS)
    chunk_of, s_of = lax.shift_right_logical(rest, 1), rest & 1
    z_of, y_of = lax.shift_right_logical(lat_of, 3), lat_of & 7
    z_first = y_of * TILE + z_of * SLOTS + s_of
    y_first = z_of * TILE + y_of * SLOTS + s_of
    column = z_first
    for c in range(CHUNKS):
        if ORIENT[c] == "y":
            column = jnp.where(chunk_of == c, y_first, column)
    column = column + chunk_of * 128
    arrive = (column == iota((degrees, degrees), 1)).astype(F32)
    loads["row"].wait()
    order_row = jnp.broadcast_to(order_row_ref[...].reshape(1, degrees).astype(F32), (8, degrees))
    order_arrive = dot(order_row, arrive, precision=HIGHEST)[0:1]
    pick_f32 = (
        iota((degrees, degrees), 0).astype(F32) == jnp.broadcast_to(order_arrive, (degrees, degrees))
    ).astype(F32)
    pick[...] = pick_f32.astype(BF16)
    pick_t = pick_f32.T.astype(BF16)

    loads["sv"].wait()
    for j in range(0, ROWS, 2):
        pair = jnp.concatenate([sv[j], sv[j + 1]], axis=1)
        moved = dot(pick_t, pair).astype(BF16)
        sv_slots[j] = moved[:, :lanes]
        sv_slots[j + 1] = moved[:, lanes:]

    turn(0)
    send_phase2(0)
    turn(1)
    send_phase2(1)
    loads["start"].wait()
    loads["width"].wait()
    first = p * ROWS
    e_row = iota((WINDOW, 128), 0)
    lane = iota((WINDOW, 128), 1)
    starts = jnp.zeros((WINDOW, 128), I32)
    widths = jnp.zeros((WINDOW, 128), I32)
    for e in range(ROWS + 2 * REACH):
        row = jnp.clip(first - REACH + e, 0, lat_rows - 1)
        starts = jnp.where(e_row == e, start_ref[row], starts)
        widths = jnp.where(e_row == e, width_ref[row], widths)
    row_e = e_row + (first - REACH)
    inside = (row_e >= 0) & (row_e < lat_rows) & (e_row < ROWS + 2 * REACH)
    widths = jnp.where(inside, widths, 0)
    row_pick = (iota((WINDOW, lat_rows), 1) == iota((WINDOW, lat_rows), 0) + (first - REACH)).astype(BF16)
    taps = dot(row_pick, filt_ref[...], ((1,), (1,)))
    tap_count = taps.shape[1]
    tap = lane + first - starts
    band = jnp.zeros((WINDOW, 128), F32)
    for t in range(tap_count):
        hit = (tap == t) & (t < widths)
        band = jnp.where(hit, jnp.broadcast_to(taps[:, t : t + 1], (WINDOW, 128)), band)
    pick_j = (lax.shift_right_logical(iota((ROWS * TILE, 128), 0), 4) == iota((ROWS * TILE, 128), 1)).astype(BF16)
    pick_e = (lax.shift_right_logical(iota((WINDOW, WINDOW * TILE), 1), 4) == iota((WINDOW, WINDOW * TILE), 0)).astype(BF16)
    wide = dot(pick_j, band.astype(BF16), ((1,), (1,))).astype(BF16)
    wide = dot(wide, pick_e)
    same_slot = (iota((ROWS * TILE, WINDOW * TILE), 0) & 15) == (iota((ROWS * TILE, WINDOW * TILE), 1) & 15)
    band_wide = jnp.where(same_slot, wide, 0.0).astype(BF16)

    for c in range(CHUNKS):
        window[c, :, ROWS + 2 * REACH : WINDOW] = jnp.zeros(
            (RING, WINDOW - ROWS - 2 * REACH, TILE, lanes), BF16
        )

    for cp in gain1:
        cp.wait_recv()
    gain_part[...] = jnp.sum(gain_got[...], axis=0)
    gain2 = []
    for n, d in enumerate(FAR_FIRST):
        cp = remote(gain_part, gain_got2.at[y], g2_send.at[n], g2_recv.at[n], y_peer(d))
        cp.start()
        gain2.append(cp)
    gain_got2[y] = gain_part[...]

    turn(2)
    send_phase2(2)
    send_halo(0)
    send_halo(1)
    for cp in gain2:
        cp.wait_recv()
    gain_mine_sum = jnp.sum(gain_got2[...], axis=0)
    gain_all[z] = gain_mine_sum
    gain3 = []
    for n, d in enumerate(FAR_FIRST):
        cp = remote(gain_all.at[z], gain_all.at[z], g3_send.at[n], g3_recv.at[n], z_peer(d))
        cp.start()
        gain3.append(cp)
    gram = jnp.zeros((WINDOW * TILE, ROWS * TILE), F32)

    def add_gram(c, gram):
        for cp in halo[c]:
            cp.wait_recv()
        tiles, sides = [], []
        for t in range(RING):
            lo = c * 128 + t * TILE
            tiles.append(window[c, t].reshape(WINDOW * TILE, lanes))
            sides.append(sv_slots[:, lo : lo + TILE, :].reshape(ROWS * TILE, lanes))
        return gram + dot(jnp.concatenate(tiles, axis=1), jnp.concatenate(sides, axis=1), ((1,), (1,)))

    def filter_rows(c):
        for t in range(RING):
            x = window[c, t].reshape(WINDOW * TILE, lanes)
            lo = c * 128 + t * TILE
            ig_slots[:, lo : lo + TILE, :] = dot(band_wide, x).astype(BF16).reshape(ROWS, TILE, lanes)

    def place_rows(j, columns):
        pair = jnp.concatenate([ig_slots[j, columns], ig_slots[j + 1, columns]], axis=1)
        return dot(pick[:, columns], pair)

    gram = add_gram(0, gram)
    filter_rows(0)
    send_halo(2)
    gram = add_gram(1, gram)
    filter_rows(1)
    early, late = slice(0, 256), slice(256, 384)
    for j in range(0, ROWS, 2):
        placed[j // 2] = place_rows(j, early)
    for cp in gain3:
        cp.wait_recv()
    for h in range(channels // 8):
        for b in range(blocks):
            gg_ref[8 * h : 8 * h + 8, 128 * b : 128 * b + 128] = gain_all[h * blocks + b]
    gram = add_gram(2, gram)

    diagonal = (iota(gram.shape, 0) & 15) == (iota(gram.shape, 1) & 15)
    gram = jnp.where(diagonal, gram, 0.0)
    by_j = (lax.shift_right_logical(iota((ROWS * TILE, 128), 0), 4) == iota((ROWS * TILE, 128), 1)).astype(F32)
    by_e = (lax.shift_right_logical(iota((WINDOW, WINDOW * TILE), 1), 4) == iota((WINDOW, WINDOW * TILE), 0)).astype(F32)
    small = dot(dot(by_e, gram, precision=HIGHEST), by_j, precision=HIGHEST)
    part = jnp.zeros((WINDOW, 128), F32)
    for j in range(ROWS):
        hit = (lane + starts == first + j) & (lane < widths)
        part = part + jnp.where(hit, jnp.broadcast_to(small[:, j : j + 1], (WINDOW, 128)), 0.0)
    filt_mine[...] = part
    filt1 = [
        remote(filt_mine, filt_got.at[0], f1_send.at[0], f1_recv.at[0], up),
        remote(filt_mine, filt_got.at[1], f1_send.at[1], f1_recv.at[1], down),
    ]
    for cp in filt1:
        cp.start()

    filter_rows(2)
    writes = []
    for j in range(0, ROWS, 2):
        if j == 2:
            for cp in filt1:
                cp.wait_recv()
            filt_sum[...] = jnp.zeros(filt_sum.shape, F32)
            filt_sum[0:ROWS] = filt_mine[REACH : REACH + ROWS]
            filt_sum[0:REACH] += filt_got[0, REACH + ROWS : ROWS + 2 * REACH]
            filt_sum[ROWS - REACH : ROWS] += filt_got[1, 0:REACH]
            filt_all[q] = filt_sum[...]
            filt2 = []
            for d in sorted(range(1, lon_count), key=lambda d: -min(d, lon_count - d)):
                cp = pltpu.make_async_remote_copy(
                    src_ref=filt_all.at[q],
                    dst_ref=filt_all.at[q],
                    send_sem=f2_send.at[d - 1],
                    recv_sem=f2_recv.at[d - 1],
                    device_id={"lon": lax.rem(q + d, lon_count)},
                    device_id_type=MESH,
                )
                cp.start()
                filt2.append(cp)
        moved = (placed[j // 2] + place_rows(j, late)).astype(BF16)
        out_rows[j] = moved[:, :lanes]
        out_rows[j + 1] = moved[:, lanes:]
        cp = pltpu.make_async_copy(
            out_rows.at[pl.ds(j, 2)], ig_hbm.at[pl.ds(j, 2)], out_sems.at[j // 2]
        )
        cp.start()
        writes.append(cp)

    for cp in filt2:
        cp.wait_recv()
    fg_ref[...] = jnp.sum(filt_all[...], axis=0)[:ROWS, :tap_count]
    for cps in [*phase1.values(), *phase2.values(), *halo.values(), gain1, gain2, gain3, filt1, filt2]:
        for cp in cps:
            cp.wait_send()
    for cp in writes:
        cp.wait()


def per_device(sv, sp, og, leg, gain, filt, start, width, order):
    lon_count = lax.axis_size("lon")
    slots, degrees, lanes = sp.shape
    rows, orders = sv.shape[0], sv.shape[1]
    lat_rows, tap_count = filt.shape
    hbm = pl.BlockSpec(memory_space=pltpu.HBM)
    vmem = pl.BlockSpec(memory_space=pltpu.VMEM)
    dma = pltpu.SemaphoreType.DMA
    peers = RING - 1
    ig, gg, fg = pl.pallas_call(
        functools.partial(kernel, lon_count),
        out_shape=(
            jax.ShapeDtypeStruct(sv.shape, BF16),
            jax.ShapeDtypeStruct(gain.shape[::-1], F32),
            jax.ShapeDtypeStruct((rows, tap_count), F32),
        ),
        in_specs=[hbm] * 4 + [vmem] * 2 + [hbm] * 3,
        out_specs=(hbm, vmem, vmem),
        scratch_shapes=[
            pltpu.VMEM(sv.shape, BF16),
            pltpu.VMEM(sp.shape, BF16),
            pltpu.VMEM(og.shape, BF16),
            pltpu.VMEM(leg.shape, BF16),
            pltpu.VMEM((CHUNKS, RING, SLOTS, PLANE, lanes), BF16),
            pltpu.VMEM((CHUNKS, RING, SLOTS, PLANE, lanes), BF16),
            pltpu.VMEM((CHUNKS, PLANE, TILE, lanes), BF16),
            pltpu.VMEM((CHUNKS, RING, WINDOW, TILE, lanes), BF16),
            pltpu.VMEM((rows, orders, lanes), BF16),
            pltpu.VMEM((rows, orders, lanes), BF16),
            pltpu.VMEM((orders, orders), BF16),
            pltpu.VMEM((rows // 2, orders, 2 * lanes), F32),
            pltpu.VMEM((rows, orders, lanes), BF16),
            pltpu.SMEM(start.shape, I32),
            pltpu.SMEM(width.shape, I32),
            pltpu.SMEM(order.shape, I32),
            pltpu.VMEM(order.shape, I32),
            pltpu.VMEM((RING, 8, 128), F32),
            pltpu.VMEM((RING, 8, 128), F32),
            pltpu.VMEM((8, 128), F32),
            pltpu.VMEM((RING, 8, 128), F32),
            pltpu.VMEM((RING, 8, 128), F32),
            pltpu.VMEM((WINDOW, 128), F32),
            pltpu.VMEM((2, WINDOW, 128), F32),
            pltpu.VMEM((16, 128), F32),
            pltpu.VMEM((lon_count, 16, 128), F32),
            dma((12,)),
            dma((rows // 2,)),
            dma((CHUNKS, peers)),
            dma((CHUNKS, peers)),
            dma((CHUNKS, peers)),
            dma((CHUNKS, peers)),
            dma((CHUNKS, 2)),
            dma((CHUNKS, 2)),
            dma((peers,)),
            dma((peers,)),
            dma((peers,)),
            dma((peers,)),
            dma((peers,)),
            dma((peers,)),
            dma((2,)),
            dma((2,)),
            dma((lon_count - 1,)),
            dma((lon_count - 1,)),
        ],
        compiler_params=pltpu.CompilerParams(
            collective_id=0, has_side_effects=True, vmem_limit_bytes=60 * 2**20
        ),
        name="backward",
    )(sv, sp, og, leg, gain.T, filt.T, start, width, order)
    return ig, gg.T, fg


def solution(mesh):
    return jax.shard_map(
        per_device,
        mesh=mesh,
        in_specs=(
            P("lat", None, "lon"),
            P("lat", None, "lon"),
            P("lat", None, "lon"),
            P("lat", None, None),
            P(None, "lon"),
            P(),
            P(),
            P(),
            P(),
        ),
        out_specs=(P("lat", None, "lon"), P(None, "lon"), P("lat", None)),
        check_vma=False,
    )
```

```python
import functools
import jax
import jax.numpy as jnp
from jax import lax
from jax.sharding import PartitionSpec as P
from jax.experimental import pallas as pl
from jax.experimental.pallas import tpu as pltpu

MESH = pl.DeviceIdType.MESH
HIGHEST = lax.Precision.HIGHEST
F32 = jnp.float32
BF16 = jnp.bfloat16
I32 = jnp.int32

RING = 8
SLOTS = 2
CHUNKS = 3
ORIENT = ("y", "z", "y")
TILE = RING * SLOTS
REACH = 6
ROWS = 10
PLANE = RING * ROWS
WINDOW = 24
FAR_FIRST = (4, 3, 5, 2, 6, 1, 7)


def iota(shape, dim):
    return lax.broadcasted_iota(I32, shape, dim)


def dot(a, b, contract=((1,), (0,)), precision=None):
    return lax.dot_general(
        a, b, (contract, ((), ())), preferred_element_type=F32, precision=precision
    )


def kernel(
    lon_count,
    sv_hbm,
    sp_hbm,
    og_hbm,
    leg_hbm,
    gain_hbm,
    filt_ref,
    start_hbm,
    width_hbm,
    order_hbm,
    ig_hbm,
    gg_ref,
    fg_ref,
    sv,
    sp,
    og,
    leg,
    sent,
    got,
    turned,
    window,
    sv_slots,
    ig_slots,
    pick,
    placed,
    out_rows,
    gain_ref,
    start_ref,
    width_ref,
    order_ref,
    order_row_ref,
    gain_mine,
    gain_got,
    gain_part,
    gain_got2,
    gain_all,
    filt_mine,
    filt_got,
    filt_sum,
    filt_all,
    load_sems,
    out_sems,
    p1_send,
    p1_recv,
    p2_send,
    p2_recv,
    halo_send,
    halo_recv,
    g1_send,
    g1_recv,
    g2_send,
    g2_recv,
    g3_send,
    g3_recv,
    f1_send,
    f1_recv,
    f2_send,
    f2_recv,
):
    p = lax.axis_index("lat")
    q = lax.axis_index("lon")
    z, y = p // RING, lax.rem(p, RING)
    lat_count = RING * RING

    def z_peer(d):
        return lax.rem(z + d, RING) * RING + y

    def y_peer(d):
        return z * RING + lax.rem(y + d, RING)

    peer_of = {"z": z_peer, "y": y_peer}
    place_of = {"z": z, "y": y}
    other = {"z": "y", "y": "z"}
    up = lax.rem(p + 1, lat_count)
    down = lax.rem(p + lat_count - 1, lat_count)

    def remote(src, dst, s, r, lat):
        return pltpu.make_async_remote_copy(
            src_ref=src,
            dst_ref=dst,
            send_sem=s,
            recv_sem=r,
            device_id={"lat": lat},
            device_id_type=MESH,
        )

    loads = {}

    def load(name, index, src, dst):
        cp = pltpu.make_async_copy(src, dst, load_sems.at[index])
        cp.start()
        loads[name] = cp

    def load_chunk(c):
        part = pl.ds(SLOTS * c, SLOTS)
        load(("og", c), 2 * c, og_hbm.at[part], og.at[part])
        load(("leg", c), 2 * c + 1, leg_hbm.at[part], leg.at[part])

    load("order", 8, order_hbm, order_ref)
    load("gain", 12, gain_hbm, gain_ref)
    load_chunk(0)

    barrier = pltpu.get_barrier_semaphore()
    for d in range(1, RING):
        for axis in ("z", "y"):
            pl.semaphore_signal(
                barrier, inc=1, device_id={"lat": peer_of[axis](d)}, device_id_type=MESH
            )
    for lat in (up, down):
        pl.semaphore_signal(barrier, inc=1, device_id={"lat": lat}, device_id_type=MESH)
    for d in range(1, lon_count):
        pl.semaphore_signal(
            barrier,
            inc=1,
            device_id={"lon": lax.rem(q + d, lon_count)},
            device_id_type=MESH,
        )

    degrees = sp.shape[1]
    lanes = sp.shape[2]
    channels = gain_hbm.shape[0]
    per_channel = lanes // channels
    lat_rows = lat_count * ROWS

    spread = (iota((channels, lanes), 1) // per_channel == iota((channels, lanes), 0)).astype(F32)
    loads["gain"].wait()
    lane_gain = dot(gain_ref[...], spread, ((0,), (0,)), precision=HIGHEST)

    degree = iota((degrees, lanes), 0)

    def turn_rows():
        row = iota((lat_rows, 128), 0)
        tens = lax.shift_right_logical(row * 6554, 16)
        rest = row - tens * ROWS
        major = lax.shift_right_logical(tens, 3)
        minor = tens & 7
        target = minor * PLANE + major * ROWS + rest
        lane = iota((lat_rows, 128), 1)
        return jnp.concatenate(
            [(target == lane + 128 * b).astype(BF16) for b in range(lat_rows // 128)], axis=1
        )

    rows_turned = turn_rows() if "y" in ORIENT else None

    def make_slot(c, s):
        k = SLOTS * c + s
        keep = degree >= order_ref[p * (SLOTS * CHUNKS) + k]
        masked = jnp.where(keep, og[k].astype(F32), 0.0)
        spec = (masked * lane_gain).astype(BF16)
        grad = dot(leg[k], spec, ((0,), (0,))).astype(BF16)
        if ORIENT[c] == "y":
            grad = dot(rows_turned, grad).astype(BF16)
        for t in range(RING):
            sent[c, t, s] = grad[t * PLANE : (t + 1) * PLANE]

    phase1 = {c: [] for c in range(CHUNKS)}
    phase2 = {}
    halo = {}

    def send_phase1(c, first, count):
        axis = ORIENT[c]
        me = place_of[axis]
        part = pl.ds(first, count)
        for n, d in enumerate(FAR_FIRST):
            target = lax.rem(me + d, RING)
            cp = remote(
                sent.at[c, target, part],
                got.at[c, me, part],
                p1_send.at[c, first, n],
                p1_recv.at[c, first, n],
                peer_of[axis](d),
            )
            cp.start()
            phase1[c].append(cp)
        for s in range(first, first + count):
            got[c, me, s] = sent[c, me, s]

    a, b = iota((256, 256), 0), iota((256, 256), 1)
    swap = ((a & 15) * 16 + lax.shift_right_logical(a, 4) == b).astype(BF16)

    def turn(c):
        for cp in phase1[c]:
            cp.wait_recv()
        for blk in range(PLANE // 16):
            x = got[c, :, :, blk * 16 : (blk + 1) * 16, :].reshape(256, lanes)
            turned[c, blk * 16 : (blk + 1) * 16] = dot(swap, x).astype(BF16).reshape(16, TILE, lanes)

    def send_phase2(c):
        axis = other[ORIENT[c]]
        me = place_of[axis]
        cps = []
        for n, d in enumerate(FAR_FIRST):
            target = lax.rem(me + d, RING)
            cp = remote(
                turned.at[c, pl.ds(target * ROWS, ROWS)],
                window.at[c, me, pl.ds(REACH, ROWS)],
                p2_send.at[c, n],
                p2_recv.at[c, n],
                peer_of[axis](d),
            )
            cp.start()
            cps.append(cp)
        window[c, me, REACH : REACH + ROWS] = turned[c, pl.ds(me * ROWS, ROWS)]
        phase2[c] = cps

    def send_halo(c):
        me = place_of[other[ORIENT[c]]]
        cps = []
        for n in range(RING):
            tile = me
            if n:
                phase2[c][n - 1].wait_recv()
                tile = lax.rem(me + RING - FAR_FIRST[n - 1], RING)
            cps += [
                remote(
                    window.at[c, tile, pl.ds(ROWS, REACH)],
                    window.at[c, tile, pl.ds(0, REACH)],
                    halo_send.at[c, 0, n],
                    halo_recv.at[c, 0, n],
                    up,
                ),
                remote(
                    window.at[c, tile, pl.ds(REACH, REACH)],
                    window.at[c, tile, pl.ds(REACH + ROWS, REACH)],
                    halo_send.at[c, 1, n],
                    halo_recv.at[c, 1, n],
                    down,
                ),
            ]
            for cp in cps[-2:]:
                cp.start()
        halo[c] = cps

    loads["order"].wait()
    loads["og", 0].wait()
    loads["leg", 0].wait()
    for c in range(1, CHUNKS):
        load_chunk(c)
    load("sp", 6, sp_hbm, sp)
    load("sv", 7, sv_hbm, sv)
    load("row", 9, order_hbm, order_row_ref)
    load("start", 10, start_hbm, start_ref)
    load("width", 11, width_hbm, width_ref)
    make_slot(0, 0)
    pl.semaphore_wait(barrier, 2 * (RING - 1) + 2 + lon_count - 1)
    send_phase1(0, 0, 1)
    make_slot(0, 1)
    send_phase1(0, 1, 1)
    for c in range(1, CHUNKS):
        loads["og", c].wait()
        loads["leg", c].wait()
        for s in range(SLOTS):
            make_slot(c, s)
        send_phase1(c, 0, SLOTS)

    loads["sp"].wait()
    total = jnp.zeros((degrees, lanes), F32)
    for k in range(SLOTS * CHUNKS):
        keep = degree >= order_ref[p * (SLOTS * CHUNKS) + k]
        masked = jnp.where(keep, og[k].astype(F32), 0.0)
        total = total + masked * sp[k].astype(F32)
    terms = dot(spread, total, ((1,), (1,)), precision=HIGHEST)
    blocks = degrees // 128
    gain_mine[...] = jnp.zeros(gain_mine.shape, F32)
    for h in range(channels // 8):
        for b in range(blocks):
            gain_mine[h * blocks + b] = terms[8 * h : 8 * h + 8, 128 * b : 128 * b + 128]
    gain1 = []
    for n, d in enumerate(FAR_FIRST):
        cp = remote(
            gain_mine.at[lax.rem(z + d, RING)], gain_got.at[z], g1_send.at[n], g1_recv.at[n], z_peer(d)
        )
        cp.start()
        gain1.append(cp)
    gain_got[z] = gain_mine[z]

    k = iota((degrees, degrees), 0)
    lat_of = lax.shift_right_logical(k * 10923, 16)
    rest = k - lat_of * (SLOTS * CHUNKS)
    chunk_of, s_of = lax.shift_right_logical(rest, 1), rest & 1
    z_of, y_of = lax.shift_right_logical(lat_of, 3), lat_of & 7
    z_first = y_of * TILE + z_of * SLOTS + s_of
    y_first = z_of * TILE + y_of * SLOTS + s_of
    column = z_first
    for c in range(CHUNKS):
        if ORIENT[c] == "y":
            column = jnp.where(chunk_of == c, y_first, column)
    column = column + chunk_of * 128
    arrive = (column == iota((degrees, degrees), 1)).astype(F32)
    loads["row"].wait()
    order_row = jnp.broadcast_to(order_row_ref[...].reshape(1, degrees).astype(F32), (8, degrees))
    order_arrive = dot(order_row, arrive, precision=HIGHEST)[0:1]
    pick_f32 = (
        iota((degrees, degrees), 0).astype(F32) == jnp.broadcast_to(order_arrive, (degrees, degrees))
    ).astype(F32)
    pick[...] = pick_f32.astype(BF16)
    pick_t = pick_f32.T.astype(BF16)

    loads["sv"].wait()
    for j in range(0, ROWS, 2):
        pair = jnp.concatenate([sv[j], sv[j + 1]], axis=1)
        moved = dot(pick_t, pair).astype(BF16)
        sv_slots[j] = moved[:, :lanes]
        sv_slots[j + 1] = moved[:, lanes:]

    turn(0)
    send_phase2(0)
    turn(1)
    send_phase2(1)
    loads["start"].wait()
    loads["width"].wait()
    first = p * ROWS
    e_row = iota((WINDOW, 128), 0)
    lane = iota((WINDOW, 128), 1)
    starts = jnp.zeros((WINDOW, 128), I32)
    widths = jnp.zeros((WINDOW, 128), I32)
    for e in range(ROWS + 2 * REACH):
        row = jnp.clip(first - REACH + e, 0, lat_rows - 1)
        starts = jnp.where(e_row == e, start_ref[row], starts)
        widths = jnp.where(e_row == e, width_ref[row], widths)
    row_e = e_row + (first - REACH)
    inside = (row_e >= 0) & (row_e < lat_rows) & (e_row < ROWS + 2 * REACH)
    widths = jnp.where(inside, widths, 0)
    row_pick = (iota((WINDOW, lat_rows), 1) == iota((WINDOW, lat_rows), 0) + (first - REACH)).astype(BF16)
    taps = dot(row_pick, filt_ref[...], ((1,), (1,)))
    tap_count = taps.shape[1]
    tap = lane + first - starts
    band = jnp.zeros((WINDOW, 128), F32)
    for t in range(tap_count):
        hit = (tap == t) & (t < widths)
        band = jnp.where(hit, jnp.broadcast_to(taps[:, t : t + 1], (WINDOW, 128)), band)
    pick_j = (lax.shift_right_logical(iota((ROWS * TILE, 128), 0), 4) == iota((ROWS * TILE, 128), 1)).astype(BF16)
    pick_e = (lax.shift_right_logical(iota((WINDOW, WINDOW * TILE), 1), 4) == iota((WINDOW, WINDOW * TILE), 0)).astype(BF16)
    wide = dot(pick_j, band.astype(BF16), ((1,), (1,))).astype(BF16)
    wide = dot(wide, pick_e)
    same_slot = (iota((ROWS * TILE, WINDOW * TILE), 0) & 15) == (iota((ROWS * TILE, WINDOW * TILE), 1) & 15)
    band_wide = jnp.where(same_slot, wide, 0.0).astype(BF16)

    for c in range(CHUNKS):
        window[c, :, ROWS + 2 * REACH : WINDOW] = jnp.zeros(
            (RING, WINDOW - ROWS - 2 * REACH, TILE, lanes), BF16
        )

    for cp in gain1:
        cp.wait_recv()
    gain_part[...] = jnp.sum(gain_got[...], axis=0)
    gain2 = []
    for n, d in enumerate(FAR_FIRST):
        cp = remote(gain_part, gain_got2.at[y], g2_send.at[n], g2_recv.at[n], y_peer(d))
        cp.start()
        gain2.append(cp)
    gain_got2[y] = gain_part[...]

    turn(2)
    send_phase2(2)
    send_halo(0)
    send_halo(1)
    for cp in gain2:
        cp.wait_recv()
    gain_mine_sum = jnp.sum(gain_got2[...], axis=0)
    gain_all[z] = gain_mine_sum
    gain3 = []
    for n, d in enumerate(FAR_FIRST):
        cp = remote(gain_all.at[z], gain_all.at[z], g3_send.at[n], g3_recv.at[n], z_peer(d))
        cp.start()
        gain3.append(cp)
    gram = jnp.zeros((WINDOW * TILE, ROWS * TILE), F32)

    def add_gram(c, gram):
        for cp in halo[c]:
            cp.wait_recv()
        tiles, sides = [], []
        for t in range(RING):
            lo = c * 128 + t * TILE
            tiles.append(window[c, t].reshape(WINDOW * TILE, lanes))
            sides.append(sv_slots[:, lo : lo + TILE, :].reshape(ROWS * TILE, lanes))
        return gram + dot(jnp.concatenate(tiles, axis=1), jnp.concatenate(sides, axis=1), ((1,), (1,)))

    def filter_rows(c):
        for t in range(RING):
            x = window[c, t].reshape(WINDOW * TILE, lanes)
            lo = c * 128 + t * TILE
            ig_slots[:, lo : lo + TILE, :] = dot(band_wide, x).astype(BF16).reshape(ROWS, TILE, lanes)

    def place_rows(j, columns):
        pair = jnp.concatenate([ig_slots[j, columns], ig_slots[j + 1, columns]], axis=1)
        return dot(pick[:, columns], pair)

    gram = add_gram(0, gram)
    filter_rows(0)
    send_halo(2)
    gram = add_gram(1, gram)
    filter_rows(1)
    early, late = slice(0, 256), slice(256, 384)
    for j in range(0, ROWS, 2):
        placed[j // 2] = place_rows(j, early)
    for cp in gain3:
        cp.wait_recv()
    for h in range(channels // 8):
        for b in range(blocks):
            gg_ref[8 * h : 8 * h + 8, 128 * b : 128 * b + 128] = gain_all[h * blocks + b]
    gram = add_gram(2, gram)

    diagonal = (iota(gram.shape, 0) & 15) == (iota(gram.shape, 1) & 15)
    gram = jnp.where(diagonal, gram, 0.0)
    by_j = (lax.shift_right_logical(iota((ROWS * TILE, 128), 0), 4) == iota((ROWS * TILE, 128), 1)).astype(F32)
    by_e = (lax.shift_right_logical(iota((WINDOW, WINDOW * TILE), 1), 4) == iota((WINDOW, WINDOW * TILE), 0)).astype(F32)
    small = dot(dot(by_e, gram, precision=HIGHEST), by_j, precision=HIGHEST)
    part = jnp.zeros((WINDOW, 128), F32)
    for j in range(ROWS):
        hit = (lane + starts == first + j) & (lane < widths)
        part = part + jnp.where(hit, jnp.broadcast_to(small[:, j : j + 1], (WINDOW, 128)), 0.0)
    filt_mine[...] = part
    filt1 = [
        remote(filt_mine, filt_got.at[0], f1_send.at[0], f1_recv.at[0], up),
        remote(filt_mine, filt_got.at[1], f1_send.at[1], f1_recv.at[1], down),
    ]
    for cp in filt1:
        cp.start()

    filter_rows(2)
    writes = []
    for j in range(0, ROWS, 2):
        if j == 2:
            for cp in filt1:
                cp.wait_recv()
            filt_sum[...] = jnp.zeros(filt_sum.shape, F32)
            filt_sum[0:ROWS] = filt_mine[REACH : REACH + ROWS]
            filt_sum[0:REACH] += filt_got[0, REACH + ROWS : ROWS + 2 * REACH]
            filt_sum[ROWS - REACH : ROWS] += filt_got[1, 0:REACH]
            filt_all[q] = filt_sum[0:8] + pltpu.roll(filt_sum[8:16], 64, 1)
            filt2 = []
            for d in sorted(range(1, lon_count), key=lambda d: -min(d, lon_count - d)):
                cp = pltpu.make_async_remote_copy(
                    src_ref=filt_all.at[q],
                    dst_ref=filt_all.at[q],
                    send_sem=f2_send.at[d - 1],
                    recv_sem=f2_recv.at[d - 1],
                    device_id={"lon": lax.rem(q + d, lon_count)},
                    device_id_type=MESH,
                )
                cp.start()
                filt2.append(cp)
        moved = (placed[j // 2] + place_rows(j, late)).astype(BF16)
        out_rows[j] = moved[:, :lanes]
        out_rows[j + 1] = moved[:, lanes:]
        cp = pltpu.make_async_copy(
            out_rows.at[pl.ds(j, 2)], ig_hbm.at[pl.ds(j, 2)], out_sems.at[j // 2]
        )
        cp.start()
        writes.append(cp)

    for cp in filt2:
        cp.wait_recv()
    filt_total = jnp.sum(filt_all[...], axis=0)
    fg_ref[0:8] = filt_total[:, :tap_count]
    fg_ref[8:ROWS] = filt_total[: ROWS - 8, 64 : 64 + tap_count]
    for cps in [*phase1.values(), *phase2.values(), *halo.values(), gain1, gain2, gain3, filt1, filt2]:
        for cp in cps:
            cp.wait_send()
    for cp in writes:
        cp.wait()


def per_device(sv, sp, og, leg, gain, filt, start, width, order):
    lon_count = lax.axis_size("lon")
    slots, degrees, lanes = sp.shape
    rows, orders = sv.shape[0], sv.shape[1]
    lat_rows, tap_count = filt.shape
    hbm = pl.BlockSpec(memory_space=pltpu.HBM)
    vmem = pl.BlockSpec(memory_space=pltpu.VMEM)
    dma = pltpu.SemaphoreType.DMA
    peers = RING - 1
    ig, gg, fg = pl.pallas_call(
        functools.partial(kernel, lon_count),
        out_shape=(
            jax.ShapeDtypeStruct(sv.shape, BF16),
            jax.ShapeDtypeStruct(gain.shape[::-1], F32),
            jax.ShapeDtypeStruct((rows, tap_count), F32),
        ),
        in_specs=[hbm] * 5 + [vmem] + [hbm] * 3,
        out_specs=(hbm, vmem, vmem),
        scratch_shapes=[
            pltpu.VMEM(sv.shape, BF16),
            pltpu.VMEM(sp.shape, BF16),
            pltpu.VMEM(og.shape, BF16),
            pltpu.VMEM(leg.shape, BF16),
            pltpu.VMEM((CHUNKS, RING, SLOTS, PLANE, lanes), BF16),
            pltpu.VMEM((CHUNKS, RING, SLOTS, PLANE, lanes), BF16),
            pltpu.VMEM((CHUNKS, PLANE, TILE, lanes), BF16),
            pltpu.VMEM((CHUNKS, RING, WINDOW, TILE, lanes), BF16),
            pltpu.VMEM((rows, orders, lanes), BF16),
            pltpu.VMEM((rows, orders, lanes), BF16),
            pltpu.VMEM((orders, orders), BF16),
            pltpu.VMEM((rows // 2, orders, 2 * lanes), F32),
            pltpu.VMEM((rows, orders, lanes), BF16),
            pltpu.VMEM(gain.shape[::-1], F32),
            pltpu.SMEM(start.shape, I32),
            pltpu.SMEM(width.shape, I32),
            pltpu.SMEM(order.shape, I32),
            pltpu.VMEM(order.shape, I32),
            pltpu.VMEM((RING, 8, 128), F32),
            pltpu.VMEM((RING, 8, 128), F32),
            pltpu.VMEM((8, 128), F32),
            pltpu.VMEM((RING, 8, 128), F32),
            pltpu.VMEM((RING, 8, 128), F32),
            pltpu.VMEM((WINDOW, 128), F32),
            pltpu.VMEM((2, WINDOW, 128), F32),
            pltpu.VMEM((16, 128), F32),
            pltpu.VMEM((lon_count, 8, 128), F32),
            dma((13,)),
            dma((rows // 2,)),
            dma((CHUNKS, SLOTS, peers)),
            dma((CHUNKS, SLOTS, peers)),
            dma((CHUNKS, peers)),
            dma((CHUNKS, peers)),
            dma((CHUNKS, 2, RING)),
            dma((CHUNKS, 2, RING)),
            dma((peers,)),
            dma((peers,)),
            dma((peers,)),
            dma((peers,)),
            dma((peers,)),
            dma((peers,)),
            dma((2,)),
            dma((2,)),
            dma((lon_count - 1,)),
            dma((lon_count - 1,)),
        ],
        compiler_params=pltpu.CompilerParams(
            collective_id=0, has_side_effects=True, vmem_limit_bytes=60 * 2**20
        ),
        name="backward",
    )(sv, sp, og, leg, gain.T, filt.T, start, width, order)
    return ig, gg.T, fg


def solution(mesh):
    return jax.shard_map(
        per_device,
        mesh=mesh,
        in_specs=(
            P("lat", None, "lon"),
            P("lat", None, "lon"),
            P("lat", None, "lon"),
            P("lat", None, None),
            P(None, "lon"),
            P(),
            P(),
            P(),
            P(),
        ),
        out_specs=(P("lat", None, "lon"), P(None, "lon"), P("lat", None)),
        check_vma=False,
    )
```
